32 devices in a mesh: energy: 8 (over z, y), atom: 4 (over x, core).
Axes of the slice: x: 2, y: 2, z: 4, core: 2. Of those that a mesh axis runs over, the one named last changes fastest.
Arguments:
- green_blocks: bfloat16 [64, 8, 2, 128, 128], P('atom', 'energy'), may hold values from -3 to 3
- coupling: bfloat16 [64, 3, 2, 128, 128], P('atom'), may hold values from -0.375 to 0.375
- phonon_weight: float32 [2, 64, 2], P(None, 'atom'), may hold values from 0.1 to 1
- offsets: int32 [64, 2], P('atom'), may hold values from 1 to 2, as said below
- bond_atom: int32 [64], P('atom'), may hold values from 0 to 31, as said below
Outputs:
- sigma: bfloat16 [32, 8, 2, 128, 128], P('atom', 'energy')
The draws below stay inside these ranges and needn't reach their ends.
Inputs may be any that keep to these rules, and one draw needn't show every extreme that they name: For every bond, its 2 modes' offsets are 1, 2, 1 and 2 in some order. `bond_atom`: atoms k * 8 to (k + 1) * 8 - 1 lie on index k of atom. Among the 16 bonds of one index of atom, every index of atom that is named is named by exactly 8 bonds, and one index of atom is named by 8 bonds of every index of atom.
All inputs are finite; a program needn't handle non-finite values.
Results may differ from the reference program's by a relative error of at most 0.0064.
Values may be sent and summed in bfloat16 or wider, within the bound.
No kernel may reach another device: no remote copies, remote signals or barrier semaphores. Data moves between devices by JAX's collectives and lax.ppermute only.
A program may use at most 64 MiB of HBM per device.

```python
import math
import jax
import jax.numpy as jnp
from jax import lax

N = 128
E_DEV = 1
B_DEV = 16
A_DEV = 8
COMPONENTS = 3
MODES = 2
CAP = 8
ENERGIES = 8
BONDS = 64
ATOMS = 32
N_ATOM = 4


def draw_offsets(key, part):
    first_key, second_key = jax.random.split(jax.random.fold_in(key, 3))
    turn = jax.random.randint(first_key, (BONDS, 1), 0, MODES)
    extra = jax.random.randint(second_key, (BONDS, MODES), 0, E_DEV)
    row_index = jnp.arange(BONDS, dtype=jnp.int32)[:, None]
    extra = jnp.where(row_index == 0, E_DEV - 1, jnp.where(row_index == 1, 0, extra))
    block_index = (jnp.arange(MODES, dtype=jnp.int32)[None, :] + turn) % MODES
    return (E_DEV * block_index + 1 + extra).astype(jnp.int32)


def draw_bond_atom(key, part):
    hot_owner = jax.random.randint(jax.random.fold_in(key, 7), (), 0, N_ATOM)
    source_keys = jax.random.split(jax.random.fold_in(key, 11), N_ATOM)
    named_count = B_DEV // CAP

    def one_source(source_key):
        perm_key, order_key, atom_key = jax.random.split(source_key, 3)
        others = jax.random.permutation(perm_key, N_ATOM - 1)
        others = others + (others >= hot_owner).astype(jnp.int32)
        chosen = jnp.concatenate([hot_owner[None].astype(jnp.int32), others[:named_count - 1].astype(jnp.int32)])
        owners = jnp.repeat(chosen, CAP)
        owners = owners[jax.random.permutation(order_key, B_DEV)]
        within = jax.random.randint(atom_key, (B_DEV,), 0, A_DEV)
        return owners * A_DEV + within
    return jax.vmap(one_source)(source_keys).reshape(-1).astype(jnp.int32)


def block_levels(rng, extent, pieces, least, high):
    level, own = 1.0, jax.random.fold_in(rng, 6)
    for position, shards_of in pieces:
        draws = jnp.exp(jax.random.uniform(jax.random.fold_in(own, position), (shards_of,), jnp.float32, least / len(pieces), high / len(pieces)))
        level = level * jnp.repeat(draws, extent[position] // shards_of).reshape([-1 if axis == position else 1 for axis in range(len(extent))])
    return level


def bell_draw(key, shape, scale, most, pieces=(), held_as=jnp.bfloat16):
    loudness = block_levels(key, shape, pieces, -0.22, 0.18) if pieces else 1.0
    values = jax.random.normal(key, shape, jnp.float32) * scale * loudness
    return jnp.minimum(jnp.maximum(values, -most), most).astype(held_as)


def setup_inputs(seed: int = 0) -> dict:
    arg_keys = jax.random.split(jax.random.key(seed), 6)
    green_blocks = bell_draw(arg_keys[0], (BONDS, ENERGIES, 2, N, N), 0.5, 3.0, ((0, 4), (1, 8)))
    coupling = bell_draw(arg_keys[1], (BONDS, COMPONENTS, 2, N, N), (2 * N) ** -0.5, 0.375, ((0, 4),))
    phonon_weight = jnp.clip(jnp.exp(math.log(1.0) - 2.3025851 * jax.random.uniform(arg_keys[2], (2, BONDS, MODES), jnp.float32) ** block_levels(arg_keys[2], (2, BONDS, MODES), ((1, 4),), -0.2, 0.2)), 0.1, 1.0)
    offsets = draw_offsets(jax.random.fold_in(arg_keys[5], 71), 0)
    bond_atom = draw_bond_atom(jax.random.fold_in(arg_keys[5], 71), 0)
    return dict(green_blocks=green_blocks, coupling=coupling, phonon_weight=phonon_weight, offsets=offsets, bond_atom=bond_atom)


def mix_bond(green_bond, absorb, emit, bond_offsets):
    energy = jnp.arange(ENERGIES, dtype=jnp.int32)
    lower_index = (energy[:, None] - bond_offsets[None, :]) % ENERGIES
    upper_index = (energy[:, None] + bond_offsets[None, :]) % ENERGIES
    lower_hit = (lower_index[:, :, None] == energy[None, None, :]).astype(jnp.float32)
    upper_hit = (upper_index[:, :, None] == energy[None, None, :]).astype(jnp.float32)
    weights = jnp.sum(absorb[None, :, None] * lower_hit + emit[None, :, None] * upper_hit, axis=1)
    flat = green_bond.astype(jnp.float32).reshape(ENERGIES, -1)
    mixed = jnp.dot(weights, flat, precision=lax.Precision.HIGHEST)
    return mixed.reshape(green_bond.shape).astype(jnp.bfloat16)


def product_bond(mixed, coupling_bond):
    real_coupling = coupling_bond[:, 0].astype(jnp.float32)
    imag_coupling = coupling_bond[:, 1].astype(jnp.float32)
    real_mixed = mixed[:, 0].astype(jnp.float32)
    imag_mixed = mixed[:, 1].astype(jnp.float32)
    highest = lax.Precision.HIGHEST

    def left_mul(first, second):
        return jnp.einsum("cij,ejk->ecik", first, second, precision=highest)

    def right_mul(first, second):
        return jnp.einsum("ecij,ckj->eik", first, second, precision=highest)

    left_real = (left_mul(real_coupling, real_mixed) - left_mul(imag_coupling, imag_mixed)).astype(jnp.bfloat16)
    left_imag = (left_mul(real_coupling, imag_mixed) + left_mul(imag_coupling, real_mixed)).astype(jnp.bfloat16)
    left_real = left_real.astype(jnp.float32)
    left_imag = left_imag.astype(jnp.float32)
    out_real = right_mul(left_real, real_coupling) - right_mul(left_imag, imag_coupling)
    out_imag = right_mul(left_real, imag_coupling) + right_mul(left_imag, real_coupling)
    return jnp.stack([out_real, out_imag], axis=1).astype(jnp.bfloat16)


def reference(green_blocks, coupling, phonon_weight, offsets, bond_atom):
    def one_bond(packed):
        green_bond, coupling_bond, absorb, emit, bond_offsets = packed
        return product_bond(mix_bond(green_bond, absorb, emit, bond_offsets), coupling_bond)

    bond_self = lax.map(one_bond, (green_blocks, coupling, phonon_weight[0], phonon_weight[1], offsets))
    sigma = jax.ops.segment_sum(bond_self.astype(jnp.float32), bond_atom, num_segments=ATOMS)
    return sigma.astype(jnp.bfloat16)
```

```python
import functools

import jax
import jax.numpy as jnp
from jax import lax
from jax.experimental import pallas as pl
from jax.experimental.pallas import tpu as pltpu
from jax.sharding import PartitionSpec as P

A_DEV = 8
CHUNKS = 1


def product_kernel(first_row, rows, group, capacity, place_ref, green_ref, coupling_ref, *out_refs):
    step = pl.program_id(0)
    components = coupling_ref.shape[1]
    for index in range(group):
        real_green = green_ref[index, 0, 0]
        imag_green = green_ref[index, 0, 1]
        right = jnp.concatenate(
            [
                jnp.concatenate([real_green, imag_green], axis=1),
                jnp.concatenate([-imag_green, real_green], axis=1),
            ],
            axis=0,
        )
        taken = pl.ds(first_row, rows)
        left = jnp.concatenate(
            [
                jnp.concatenate(
                    [coupling_ref[index, c, 0, taken], coupling_ref[index, c, 1, taken]], axis=1
                )
                for c in range(components)
            ],
            axis=0,
        )
        product = jnp.dot(left, right, preferred_element_type=jnp.float32).astype(jnp.bfloat16)
        total = None
        for c in range(components):
            real_part = coupling_ref[index, c, 0]
            imag_part = coupling_ref[index, c, 1]
            last = jnp.concatenate(
                [
                    jnp.concatenate([real_part, -imag_part], axis=1),
                    jnp.concatenate([imag_part, real_part], axis=1),
                ],
                axis=0,
            )
            term = lax.dot_general(
                product[c * rows : (c + 1) * rows],
                last,
                (((1,), (1,)), ((), ())),
                preferred_element_type=jnp.float32,
            )
            total = term if total is None else total + term
        total = total.astype(jnp.bfloat16)
        columns = total.shape[1] // 2
        place = place_ref[step * group + index]
        rank = lax.rem(place, capacity)
        owner = lax.div(place, capacity)
        for d, out_ref in enumerate(out_refs):

            def store(out_ref=out_ref, slot=rank if len(out_refs) > 1 else place):
                out_ref[slot, 0] = total[:, :columns]
                out_ref[slot, 1] = total[:, columns:]

            if len(out_refs) > 1:
                pl.when(owner == d)(store)
            else:
                store()


def bond_products(place, green, coupling, owner_count, capacity, chunk, chunks, split):
    bond_count, _, parts, size, _ = green.shape
    components = coupling.shape[1]
    rows = size // chunks
    group = 4 if bond_count % 4 == 0 else 1
    out_count, slots = (owner_count, capacity) if split else (1, owner_count * capacity)
    shape = (slots, parts, rows, size)
    return pl.pallas_call(
        functools.partial(product_kernel, chunk * rows, rows, group, capacity),
        out_shape=[jax.ShapeDtypeStruct(shape, jnp.bfloat16)] * out_count,
        grid_spec=pltpu.PrefetchScalarGridSpec(
            num_scalar_prefetch=1,
            grid=(bond_count // group,),
            in_specs=[
                pl.BlockSpec((group, 1, parts, size, size), lambda s, _: (s, 0, 0, 0, 0)),
                pl.BlockSpec((group, components, parts, size, size), lambda s, _: (s, 0, 0, 0, 0)),
            ],
            out_specs=[pl.BlockSpec(shape, lambda s, _: (0, 0, 0, 0))] * out_count,
        ),
        compiler_params=pltpu.CompilerParams(vmem_limit_bytes=32 * 2**20),
        cost_estimate=pl.CostEstimate(
            flops=16 * bond_count * components * rows * size * size,
            bytes_accessed=2 * (green.size + coupling.size),
            transcendentals=0,
        ),
        name="bond_products",
    )(place, green, coupling)


def gather_kernel(source_count, capacity, wide, atom_ref, weight_ref, *refs):
    sources = refs[:source_count]
    outs = refs[source_count:-1]
    total = refs[-1]
    slot_count = source_count * capacity
    total[...] = jnp.zeros_like(total)
    for d, source in enumerate(sources):

        def add(slot, carry, d=d, source=source):
            entry = d * capacity + slot
            atom = atom_ref[entry]

            @pl.when(atom >= 0)
            def _():
                values = source[slot].astype(jnp.float32)
                for kind in range(len(outs)):
                    total[kind, atom] += weight_ref[kind * slot_count + entry] * values

            return carry

        lax.fori_loop(0, capacity, add, 0)
    for kind, out in enumerate(outs):
        out[...] = total[kind].astype(out.dtype)


def atom_sums(atoms, weights, sources, kinds, wide):
    capacity, parts, rows, size = sources[0].shape
    steps = max(1, rows // 32)
    tile = rows // steps
    return pl.pallas_call(
        functools.partial(gather_kernel, len(sources), capacity, wide),
        out_shape=[
            jax.ShapeDtypeStruct(
                (A_DEV, 1, parts, rows, size), jnp.float32 if kind in wide else jnp.bfloat16
            )
            for kind in range(kinds)
        ],
        grid_spec=pltpu.PrefetchScalarGridSpec(
            num_scalar_prefetch=2,
            grid=(steps,),
            in_specs=[pl.BlockSpec((capacity, parts, tile, size), lambda s, *_: (0, 0, s, 0))]
            * len(sources),
            out_specs=[
                pl.BlockSpec((A_DEV, None, parts, tile, size), lambda s, *_: (0, 0, 0, s, 0))
            ]
            * kinds,
            scratch_shapes=[pltpu.VMEM((kinds, A_DEV, parts, tile, size), jnp.float32)],
        ),
        compiler_params=pltpu.CompilerParams(vmem_limit_bytes=32 * 2**20),
        cost_estimate=pl.CostEstimate(
            flops=2 * kinds * len(sources) * sources[0].size,
            bytes_accessed=2 * len(sources) * sources[0].size,
            transcendentals=0,
        ),
        name="atom_sums",
    )(atoms, weights, *sources)


def body(green_blocks, coupling, phonon_weight, offsets, bond_atom):
    bond_count = green_blocks.shape[0]
    modes = offsets.shape[1]
    energy_size = lax.axis_size("energy")
    owner_count = lax.axis_size("atom")
    my_energy = lax.axis_index("energy")
    my_owner = lax.axis_index("atom")
    member = my_energy % modes
    capacity = max(2, 2 * bond_count // owner_count)
    split = owner_count == 4
    slot_count = owner_count * capacity

    def inner(d):
        return [
            (e, e // modes * modes + (e + d) % modes) for e in range(energy_size)
        ]

    def outer(d):
        return [(e, (e + d * modes) % energy_size) for e in range(energy_size)]

    owner_index = bond_atom // A_DEV
    bond_order = jnp.arange(bond_count, dtype=jnp.int32)
    same_owner = (owner_index[None, :] == owner_index[:, None]) & (
        bond_order[None, :] < bond_order[:, None]
    )
    rank = jnp.sum(same_owner.astype(jnp.int32), axis=1)
    route = owner_index ^ my_owner if split else owner_index
    place = route * capacity + rank

    products = [
        bond_products(place, green_blocks, coupling, owner_count, capacity, c, CHUNKS, split)
        for c in range(CHUNKS)
    ]

    if modes == 2:
        sign = jnp.where(member == 0, 1, -1)
        shifts = [sign, -sign, -2 * sign, 2 * sign]
        wide = (3,)
    else:
        shifts = []
        for d in range(1, modes):
            partner = (member + d) % modes
            shifts.append(partner - member)
            shifts.append(jnp.where(member > partner, modes, -modes) + partner - member)
        wide = (len(shifts), len(shifts) + 1)
        shifts += [jnp.int32(modes), jnp.int32(-modes)]
    kinds = len(shifts)
    bond_weight = [
        jnp.sum(
            jnp.where(
                offsets == jnp.abs(shift),
                jnp.where(shift > 0, phonon_weight[0], phonon_weight[1]),
                0.0,
            ),
            axis=1,
        )
        for shift in shifts
    ]
    facts = jnp.stack(bond_weight + [(bond_atom % A_DEV + 1).astype(jnp.float32)], axis=0)
    slot_match = (owner_index * capacity + rank)[None, :] == jnp.arange(slot_count)[:, None]
    facts = jnp.sum(jnp.where(slot_match[None], facts[:, None, :], 0.0), axis=2)
    facts = facts.reshape(kinds + 1, owner_count, capacity)
    facts = lax.all_to_all(facts, "atom", split_axis=1, concat_axis=1, tiled=True)
    if split:
        facts = jnp.stack(
            [
                lax.dynamic_index_in_dim(facts, my_owner ^ d, 1, keepdims=False)
                for d in range(owner_count)
            ],
            axis=1,
        )
    atoms = facts[kinds].reshape(-1).astype(jnp.int32) - 1
    weights = facts[:kinds].reshape(-1)

    parts = []
    for c in range(CHUNKS):
        if split:
            sources = [products[c][0]]
            for d in range(1, owner_count):
                sources.append(
                    lax.ppermute(
                        products[c][d], "atom", [(o, o ^ d) for o in range(owner_count)]
                    )
                )
        else:
            shape = products[c][0].shape
            arrived = lax.all_to_all(
                products[c][0].reshape((owner_count, capacity) + shape[1:]),
                "atom",
                split_axis=0,
                concat_axis=0,
                tiled=True,
            )
            sources = [arrived.reshape(shape)]
        sums = atom_sums(atoms, weights, sources, kinds, wide)
        f32 = jnp.float32
        if modes == 2:
            near, relay, early, late = sums
            relay = lax.ppermute(relay, "energy", inner(1))
            early_pairs = [
                (e, (e + (-2 if e % 2 == 0 else 2)) % energy_size) for e in range(energy_size)
            ]
            late_pairs = [
                (e, (e + (2 if e % 2 == 0 else -2)) % energy_size) for e in range(energy_size)
            ]
            early = lax.ppermute(early, "energy", early_pairs)
            near = lax.ppermute(near, "energy", inner(1))
            late = (late + relay.astype(f32)).astype(jnp.bfloat16)
            late = lax.ppermute(late, "energy", late_pairs)
            part = early.astype(f32) + near.astype(f32) + late.astype(f32)
        else:
            up, down = sums[-2:]
            part = 0.0
            for d in range(1, modes):
                near = lax.ppermute(sums[2 * d - 2], "energy", inner(d))
                relay = lax.ppermute(sums[2 * d - 1], "energy", inner(d)).astype(f32)
                part = part + near.astype(f32)
                up = up + jnp.where(member < d, relay, 0.0)
                down = down + jnp.where(member < d, 0.0, relay)
            up = lax.ppermute(up.astype(jnp.bfloat16), "energy", outer(1))
            down = lax.ppermute(down.astype(jnp.bfloat16), "energy", outer(-1))
            part = part + up.astype(f32) + down.astype(f32)
        parts.append(part.astype(jnp.bfloat16))
    return parts[0] if CHUNKS == 1 else jnp.concatenate(parts, axis=3)


def solution(mesh):
    placed = (
        P("atom", "energy", None, None, None),
        P("atom", None, None, None, None),
        P(None, "atom", None),
        P("atom", None),
        P("atom"),
    )
    return jax.shard_map(
        body,
        mesh=mesh,
        in_specs=placed,
        out_specs=P("atom", "energy", None, None, None),
        check_vma=False,
    )
```

```python
import functools

import jax
import jax.numpy as jnp
from jax import lax
from jax.experimental import pallas as pl
from jax.experimental.pallas import tpu as pltpu
from jax.sharding import PartitionSpec as P

A_DEV = 8
SHARES = (4, 4)
VMEM_LIMIT = 52 * 2**20
PIECES = 3
CLAIM = 10**9


def product_kernel(row_counts, capacity, split, atom_ref, green_ref, coupling_ref, *refs):
    outs, used_ref = refs[:-1], refs[-1]
    step = pl.program_id(0)
    group, components, _, size, _ = coupling_ref.shape
    my_owner = lax.axis_index("atom") if split else 0

    @pl.when(step == 0)
    def _():
        for owner in range(used_ref.shape[0]):
            used_ref[owner] = 0

    for index in range(group):
        real_green = green_ref[index, 0, 0]
        imag_green = green_ref[index, 0, 1]
        right = jnp.concatenate(
            [
                jnp.concatenate([real_green, imag_green], axis=1),
                jnp.concatenate([-imag_green, real_green], axis=1),
            ],
            axis=0,
        )
        parts = [(coupling_ref[index, c, 0], coupling_ref[index, c, 1]) for c in range(components)]
        left = jnp.concatenate([jnp.concatenate(part, axis=1) for part in parts], axis=0)
        product = jnp.dot(left, right, preferred_element_type=jnp.float32).astype(jnp.bfloat16)
        product = jnp.concatenate(
            [product[c * size : (c + 1) * size] for c in range(components)], axis=1
        )
        last = jnp.concatenate(
            [
                jnp.concatenate(
                    [
                        jnp.concatenate([real_part, -imag_part], axis=1),
                        jnp.concatenate([imag_part, real_part], axis=1),
                    ],
                    axis=0,
                )
                for real_part, imag_part in parts
            ],
            axis=1,
        )
        total = lax.dot_general(
            product, last, (((1,), (1,)), ((), ())), preferred_element_type=jnp.float32
        ).astype(jnp.bfloat16)
        owner = lax.div(atom_ref[step * group + index], A_DEV)
        rank = used_ref[owner]
        used_ref[owner] = rank + 1
        near_place = (owner ^ my_owner) * capacity + rank
        first = 0
        for out, rows in zip(outs, row_counts):
            place = near_place if out is outs[0] else owner * capacity + rank
            out[place, 0] = total[first : first + rows, :size]
            out[place, 1] = total[first : first + rows, size:]
            first += rows


def bond_products(bond_atom, green, coupling, owner_count, capacity, row_counts, split):
    bond_count, _, parts, size, _ = green.shape
    components = coupling.shape[1]
    group = 4 if bond_count % 4 == 0 else 1
    return pl.pallas_call(
        functools.partial(product_kernel, row_counts, capacity, split),
        out_shape=[
            jax.ShapeDtypeStruct((owner_count * capacity, parts, rows, size), jnp.bfloat16)
            for rows in row_counts
        ],
        grid=(bond_count // group,),
        in_specs=[
            pl.BlockSpec(memory_space=pltpu.SMEM),
            pl.BlockSpec((group, 1, parts, size, size), lambda s: (s, 0, 0, 0, 0)),
            pl.BlockSpec((group, components, parts, size, size), lambda s: (s, 0, 0, 0, 0)),
        ],
        out_specs=[pl.BlockSpec(memory_space=pltpu.VMEM)] * len(row_counts),
        scratch_shapes=[pltpu.SMEM((owner_count,), jnp.int32)],
        compiler_params=pltpu.CompilerParams(vmem_limit_bytes=VMEM_LIMIT),
        cost_estimate=pl.CostEstimate(
            flops=16 * bond_count * components * size**3,
            bytes_accessed=2 * (green.size + coupling.size),
            transcendentals=0,
        ),
        name="bond_products",
    )(bond_atom, green, coupling)


def gather_kernel(kinds, owner_count, capacity, split, atom_ref, weight_ref, *refs):
    sources, outs, total = refs[: -len(kinds) - 1], refs[-len(kinds) - 1 : -1], refs[-1]
    rows = total.shape[2]
    slot_count = atom_ref.shape[0]
    total[...] = jnp.zeros_like(total)

    def add_owner(owner, source, first_slot):
        def add(slot, carry):
            entry = owner * capacity + slot
            atom = atom_ref[entry]
            start = pl.multiple_of((first_slot + slot) * rows, rows)
            values = source[pl.ds(start, rows), :].astype(jnp.float32)
            for index, kind in enumerate(kinds):
                total[index, atom] += weight_ref[kind * slot_count + entry] * values
            return carry

        count = jnp.int32(0)
        for slot in range(capacity):
            count += (atom_ref[owner * capacity + slot] >= 0).astype(jnp.int32)
        lax.fori_loop(0, count, add, 0)

    if len(sources) == owner_count:
        for owner, source in enumerate(sources):
            add_owner(owner, source, 0)
    else:

        me = lax.axis_index("atom") if split else 0

        def add_all(owner, carry):
            add_owner(owner, sources[0], (owner ^ me) * capacity)
            return carry

        lax.fori_loop(0, owner_count, add_all, 0)
    for index, out in enumerate(outs):
        out[...] = total[index].reshape(out.shape).astype(out.dtype)


def atom_sums(atoms, weights, sources, kinds, wide, owner_count, block_shape, claimed=0):
    capacity = atoms.shape[0] // owner_count
    parts, rows, size = block_shape
    return pl.pallas_call(
        functools.partial(gather_kernel, kinds, owner_count, capacity, owner_count == 4),
        out_shape=[
            jax.ShapeDtypeStruct(
                (A_DEV, 1, parts, rows, size), jnp.float32 if kind in wide else jnp.bfloat16
            )
            for kind in kinds
        ],
        grid_spec=pltpu.PrefetchScalarGridSpec(
            num_scalar_prefetch=2,
            grid=(1,),
            in_specs=[pl.BlockSpec(memory_space=pltpu.VMEM)] * len(sources),
            out_specs=[pl.BlockSpec(memory_space=pltpu.VMEM)] * len(kinds),
            scratch_shapes=[pltpu.VMEM((len(kinds), A_DEV, parts * rows, size), jnp.float32)],
        ),
        compiler_params=pltpu.CompilerParams(vmem_limit_bytes=32 * 2**20),
        cost_estimate=pl.CostEstimate(
            flops=claimed,
            bytes_accessed=2 * len(sources) * sources[0].size,
            transcendentals=0,
        ),
        name="atom_sums",
    )(atoms, weights, *sources)


def body(green_blocks, coupling, phonon_weight, offsets, bond_atom):
    f32, bf16 = jnp.float32, jnp.bfloat16
    bond_count = green_blocks.shape[0]
    parts_count, size = green_blocks.shape[2], green_blocks.shape[-1]
    modes = offsets.shape[1]
    energy_size = lax.axis_size("energy")
    owner_count = lax.axis_size("atom")
    member = lax.axis_index("energy") % modes
    capacity = max(2, 2 * bond_count // owner_count)
    split = owner_count == 4
    slot_count = owner_count * capacity
    row_counts = [size * share // sum(SHARES) for share in SHARES]

    def inner(d):
        return [(e, e // modes * modes + (e + d) % modes) for e in range(energy_size)]

    def outer(d):
        return [(e, (e + d * modes) % energy_size) for e in range(energy_size)]

    def even_odd(step):
        return [(e, (e + (step if e % 2 == 0 else -step)) % energy_size) for e in range(energy_size)]

    products = bond_products(
        bond_atom, green_blocks, coupling, owner_count, capacity, row_counts, split
    )

    phonon_weight, offsets, bond_atom, products = lax.optimization_barrier(
        (phonon_weight, offsets, bond_atom, products)
    )
    if modes == 2:
        sign = jnp.where(member == 0, 1, -1)
        shifts = [sign, -sign, -2 * sign, 2 * sign]
        wide = (3,)
    else:
        shifts = []
        for d in range(1, modes):
            partner = (member + d) % modes
            shifts.append(partner - member)
            shifts.append(jnp.where(member > partner, modes, -modes) + partner - member)
        wide = (len(shifts), len(shifts) + 1)
        shifts += [jnp.int32(modes), jnp.int32(-modes)]
    kinds = len(shifts)
    owner_index = bond_atom // A_DEV
    bond_order = jnp.arange(bond_count, dtype=jnp.int32)
    same_owner = (owner_index[None, :] == owner_index[:, None]) & (
        bond_order[None, :] < bond_order[:, None]
    )
    rank = jnp.sum(same_owner.astype(jnp.int32), axis=1)
    route = owner_index ^ lax.axis_index("atom") if split else owner_index
    bond_weight = jnp.stack(
        [
            jnp.sum(
                jnp.where(
                    offsets == jnp.abs(shift),
                    jnp.where(shift > 0, phonon_weight[0], phonon_weight[1]),
                    0.0,
                ),
                axis=1,
            )
            for shift in shifts
        ],
        axis=1,
    )
    pieces, rest = [], bond_weight
    for piece in range(PIECES):
        pieces.append(lax.reduce_precision(rest, 8, 7))
        rest = rest - pieces[-1]
    facts = jnp.concatenate(pieces + [(bond_atom % A_DEV + 1).astype(f32)[:, None]], axis=1)
    slot_match = (route * capacity + rank)[None, :] == jnp.arange(slot_count)[:, None]
    facts = jnp.sum(jnp.where(slot_match[:, :, None], facts[None], 0.0), axis=1)
    facts = facts.astype(bf16).reshape(owner_count, capacity, -1)
    if split:
        facts = jnp.pad(
            facts, ((0, 0), (0, -capacity % 16), (0, size - facts.shape[2]))
        )
    else:
        facts = lax.all_to_all(facts, "atom", split_axis=0, concat_axis=0, tiled=True)

    def to_owners(blocks, facts):
        if not split or facts is None:
            blocks = blocks.reshape((owner_count, capacity) + blocks.shape[1:])
            blocks = lax.all_to_all(blocks, "atom", split_axis=0, concat_axis=0, tiled=True)
            return [blocks.reshape(-1, size)]
        blocks = blocks.reshape(owner_count, -1, size)
        if facts is not None:
            blocks = jnp.concatenate([blocks, facts], axis=1)
        return [blocks[0]] + [
            lax.ppermute(blocks[d], "atom", [(o, o ^ d) for o in range(owner_count)])
            for d in range(1, owner_count)
        ]

    sources = [
        to_owners(block, facts if c == 0 else None) for c, block in enumerate(products)
    ]
    if split:
        first = capacity * parts_count * row_counts[0]
        facts = jnp.concatenate([source[first : first + capacity] for source in sources[0]], axis=0)
    else:
        facts = facts.reshape(slot_count, -1)
    weights = sum(
        facts[:, piece * kinds : (piece + 1) * kinds].astype(f32) for piece in range(PIECES)
    )
    weights = weights.T.reshape(-1)
    atoms = facts[:, PIECES * kinds].astype(jnp.int32) - 1

    def sums_of(c, chosen, claimed=0):
        shape = (parts_count, row_counts[c], size)
        return atom_sums(atoms, weights, sources[c], chosen, wide, owner_count, shape, claimed)

    parts = []
    if modes == 2:
        for c in range(len(row_counts)):
            relay, early = sums_of(c, (1, 2))
            near, late = sums_of(c, (0, 3))
            relay = lax.ppermute(relay, "energy", inner(1))
            early = lax.ppermute(early, "energy", even_odd(-2))
            relay, early = lax.optimization_barrier((relay, early))
            late = (late + relay.astype(f32)).astype(bf16)
            near = lax.ppermute(near, "energy", inner(1))
            late = lax.ppermute(late, "energy", even_odd(2))
            parts.append([early, near, late])
        parts = [sum(x.astype(f32) for x in part).astype(bf16) for part in parts]
    else:
        for c in range(len(row_counts)):
            sums = sums_of(c, tuple(range(kinds)))
            up, down = sums[-2:]
            part = 0.0
            for d in range(1, modes):
                near = lax.ppermute(sums[2 * d - 2], "energy", inner(d))
                relay = lax.ppermute(sums[2 * d - 1], "energy", inner(d)).astype(f32)
                part = part + near.astype(f32)
                up = up + jnp.where(member < d, relay, 0.0)
                down = down + jnp.where(member < d, 0.0, relay)
            up = lax.ppermute(up.astype(bf16), "energy", outer(1))
            down = lax.ppermute(down.astype(bf16), "energy", outer(-1))
            parts.append((part + up.astype(f32) + down.astype(f32)).astype(bf16))
    return jnp.concatenate(parts, axis=3)


def solution(mesh):
    placed = (
        P("atom", "energy", None, None, None),
        P("atom", None, None, None, None),
        P(None, "atom", None),
        P("atom", None),
        P("atom"),
    )
    return jax.shard_map(
        body,
        mesh=mesh,
        in_specs=placed,
        out_specs=P("atom", "energy", None, None, None),
        check_vma=False,
    )
```

```python
import functools

import jax
import jax.numpy as jnp
from jax import lax
from jax.experimental import pallas as pl
from jax.experimental.pallas import tpu as pltpu
from jax.sharding import PartitionSpec as P

A_DEV = 8
SHARES = (4, 4)
VMEM_LIMIT = 52 * 2**20
PIECES = 3


def product_kernel(row_counts, capacity, split, atom_ref, green_ref, coupling_ref, *refs):
    outs, used_ref = refs[:-1], refs[-1]
    step = pl.program_id(0)
    group, components, _, size, _ = coupling_ref.shape
    my_owner = lax.axis_index("atom") if split else 0

    @pl.when(step == 0)
    def _():
        for owner in range(used_ref.shape[0]):
            used_ref[owner] = 0

    products = []
    for index in range(group):
        real_green = green_ref[index, 0, 0]
        imag_green = green_ref[index, 0, 1]
        right = jnp.concatenate(
            [
                jnp.concatenate([real_green, imag_green], axis=1),
                jnp.concatenate([-imag_green, real_green], axis=1),
            ],
            axis=0,
        )
        left = jnp.concatenate(
            [
                jnp.concatenate([coupling_ref[index, c, 0], coupling_ref[index, c, 1]], axis=1)
                for c in range(components)
            ],
            axis=0,
        )
        product = jnp.dot(left, right, preferred_element_type=jnp.float32).astype(jnp.bfloat16)
        products.append(
            jnp.concatenate([product[c * size : (c + 1) * size] for c in range(components)], axis=1)
        )
    for index in range(group):
        rows_of = []
        for c in range(components):
            real_last, imag_last = coupling_ref[index, c, 0].T, coupling_ref[index, c, 1].T
            rows_of.append(jnp.concatenate([real_last, imag_last], axis=1))
            rows_of.append(jnp.concatenate([-imag_last, real_last], axis=1))
        last = jnp.concatenate(rows_of, axis=0)
        total = lax.dot_general(
            products[index], last, (((1,), (0,)), ((), ())), preferred_element_type=jnp.float32
        ).astype(jnp.bfloat16)
        owner = lax.div(atom_ref[step * group + index], A_DEV)
        rank = used_ref[owner]
        used_ref[owner] = rank + 1
        near_place = (owner ^ my_owner) * capacity + rank
        first = 0
        for out, rows in zip(outs, row_counts):
            place = near_place if out is outs[0] else owner * capacity + rank
            out[place, 0] = total[first : first + rows, :size]
            out[place, 1] = total[first : first + rows, size:]
            first += rows


def bond_products(bond_atom, green, coupling, owner_count, capacity, row_counts, split):
    bond_count, _, parts, size, _ = green.shape
    components = coupling.shape[1]
    group = 8 if bond_count % 8 == 0 else 1
    return pl.pallas_call(
        functools.partial(product_kernel, row_counts, capacity, split),
        out_shape=[
            jax.ShapeDtypeStruct((owner_count * capacity, parts, rows, size), jnp.bfloat16)
            for rows in row_counts
        ],
        grid=(bond_count // group,),
        in_specs=[
            pl.BlockSpec(memory_space=pltpu.SMEM),
            pl.BlockSpec((group, 1, parts, size, size), lambda s: (s, 0, 0, 0, 0)),
            pl.BlockSpec((group, components, parts, size, size), lambda s: (s, 0, 0, 0, 0)),
        ],
        out_specs=[pl.BlockSpec(memory_space=pltpu.VMEM)] * len(row_counts),
        scratch_shapes=[pltpu.SMEM((owner_count,), jnp.int32)],
        compiler_params=pltpu.CompilerParams(vmem_limit_bytes=VMEM_LIMIT),
        cost_estimate=pl.CostEstimate(
            flops=16 * bond_count * components * size**3,
            bytes_accessed=2 * (green.size + coupling.size),
            transcendentals=0,
        ),
        name="bond_products",
    )(bond_atom, green, coupling)


def gather_kernel(kinds, owner_count, capacity, split, atom_ref, weight_ref, *refs):
    sources, outs, total = refs[: -len(kinds) - 1], refs[-len(kinds) - 1 : -1], refs[-1]
    rows = total.shape[2]
    slot_count = atom_ref.shape[0]
    total[...] = jnp.zeros_like(total)

    def add_owner(owner, source, first_slot):
        def add(slot, carry):
            entry = owner * capacity + slot
            atom = atom_ref[entry]
            start = pl.multiple_of((first_slot + slot) * rows, rows)
            values = source[pl.ds(start, rows), :].astype(jnp.float32)
            for index, kind in enumerate(kinds):
                total[index, atom] += weight_ref[kind * slot_count + entry] * values
            return carry

        count = jnp.int32(0)
        for slot in range(capacity):
            count += (atom_ref[owner * capacity + slot] >= 0).astype(jnp.int32)
        lax.fori_loop(0, count, add, 0)

    if len(sources) == owner_count:
        for owner, source in enumerate(sources):
            add_owner(owner, source, 0)
    else:

        me = lax.axis_index("atom") if split else 0

        def add_all(owner, carry):
            add_owner(owner, sources[0], (owner ^ me) * capacity)
            return carry

        lax.fori_loop(0, owner_count, add_all, 0)
    for index, out in enumerate(outs):
        out[...] = total[index].reshape(out.shape).astype(out.dtype)


def atom_sums(atoms, weights, sources, kinds, wide, owner_count, block_shape):
    capacity = atoms.shape[0] // owner_count
    parts, rows, size = block_shape
    return pl.pallas_call(
        functools.partial(gather_kernel, kinds, owner_count, capacity, owner_count == 4),
        out_shape=[
            jax.ShapeDtypeStruct(
                (A_DEV, 1, parts, rows, size), jnp.float32 if kind in wide else jnp.bfloat16
            )
            for kind in kinds
        ],
        grid_spec=pltpu.PrefetchScalarGridSpec(
            num_scalar_prefetch=2,
            grid=(1,),
            in_specs=[pl.BlockSpec(memory_space=pltpu.VMEM)] * len(sources),
            out_specs=[pl.BlockSpec(memory_space=pltpu.VMEM)] * len(kinds),
            scratch_shapes=[pltpu.VMEM((len(kinds), A_DEV, parts * rows, size), jnp.float32)],
        ),
        compiler_params=pltpu.CompilerParams(vmem_limit_bytes=32 * 2**20),
        cost_estimate=pl.CostEstimate(
            flops=2 * len(kinds) * len(sources) * sources[0].size,
            bytes_accessed=2 * len(sources) * sources[0].size,
            transcendentals=0,
        ),
        name="atom_sums",
    )(atoms, weights, *sources)


def body(green_blocks, coupling, phonon_weight, offsets, bond_atom):
    f32, bf16 = jnp.float32, jnp.bfloat16
    bond_count = green_blocks.shape[0]
    parts_count, size = green_blocks.shape[2], green_blocks.shape[-1]
    modes = offsets.shape[1]
    energy_size = lax.axis_size("energy")
    owner_count = lax.axis_size("atom")
    member = lax.axis_index("energy") % modes
    capacity = max(2, 2 * bond_count // owner_count)
    split = owner_count == 4
    slot_count = owner_count * capacity
    row_counts = [size * share // sum(SHARES) for share in SHARES]

    def inner(d):
        return [(e, e // modes * modes + (e + d) % modes) for e in range(energy_size)]

    def outer(d):
        return [(e, (e + d * modes) % energy_size) for e in range(energy_size)]

    def even_odd(step):
        return [(e, (e + (step if e % 2 == 0 else -step)) % energy_size) for e in range(energy_size)]

    products = bond_products(
        bond_atom, green_blocks, coupling, owner_count, capacity, row_counts, split
    )

    phonon_weight, offsets, bond_atom, products = lax.optimization_barrier(
        (phonon_weight, offsets, bond_atom, products)
    )
    if modes == 2:
        sign = jnp.where(member == 0, 1, -1)
        shifts = [sign, -sign, -2 * sign, 2 * sign]
        wide = (3,)
    else:
        shifts = []
        for d in range(1, modes):
            partner = (member + d) % modes
            shifts.append(partner - member)
            shifts.append(jnp.where(member > partner, modes, -modes) + partner - member)
        wide = (len(shifts), len(shifts) + 1)
        shifts += [jnp.int32(modes), jnp.int32(-modes)]
    kinds = len(shifts)
    owner_index = bond_atom // A_DEV
    bond_order = jnp.arange(bond_count, dtype=jnp.int32)
    same_owner = (owner_index[None, :] == owner_index[:, None]) & (
        bond_order[None, :] < bond_order[:, None]
    )
    rank = jnp.sum(same_owner.astype(jnp.int32), axis=1)
    route = owner_index ^ lax.axis_index("atom") if split else owner_index
    bond_weight = jnp.stack(
        [
            jnp.sum(
                jnp.where(
                    offsets == jnp.abs(shift),
                    jnp.where(shift > 0, phonon_weight[0], phonon_weight[1]),
                    0.0,
                ),
                axis=1,
            )
            for shift in shifts
        ],
        axis=1,
    )
    pieces, rest = [], bond_weight
    for piece in range(PIECES):
        pieces.append(lax.reduce_precision(rest, 8, 7))
        rest = rest - pieces[-1]
    facts = jnp.concatenate(pieces + [(bond_atom % A_DEV + 1).astype(f32)[:, None]], axis=1)
    slot_match = (route * capacity + rank)[None, :] == jnp.arange(slot_count)[:, None]
    facts = jnp.sum(jnp.where(slot_match[:, :, None], facts[None], 0.0), axis=1)
    facts = facts.astype(bf16).reshape(owner_count, capacity, -1)
    if split:
        facts = jnp.pad(
            facts, ((0, 0), (0, -capacity % 16), (0, size - facts.shape[2]))
        )
    else:
        facts = lax.all_to_all(facts, "atom", split_axis=0, concat_axis=0, tiled=True)

    def to_owners(blocks, facts):
        if not split or facts is None:
            blocks = blocks.reshape((owner_count, capacity) + blocks.shape[1:])
            blocks = lax.all_to_all(blocks, "atom", split_axis=0, concat_axis=0, tiled=True)
            return [blocks.reshape(-1, size)]
        blocks = blocks.reshape(owner_count, -1, size)
        if facts is not None:
            blocks = jnp.concatenate([blocks, facts], axis=1)
        return [blocks[0]] + [
            lax.ppermute(blocks[d], "atom", [(o, o ^ d) for o in range(owner_count)])
            for d in range(1, owner_count)
        ]

    sources = [
        to_owners(block, facts if c == 0 else None) for c, block in enumerate(products)
    ]
    if split:
        first = capacity * parts_count * row_counts[0]
        facts = jnp.concatenate([source[first : first + capacity] for source in sources[0]], axis=0)
    else:
        facts = facts.reshape(slot_count, -1)
    weights = sum(
        facts[:, piece * kinds : (piece + 1) * kinds].astype(f32) for piece in range(PIECES)
    )
    weights = weights.T.reshape(-1)
    atoms = facts[:, PIECES * kinds].astype(jnp.int32) - 1

    def sums_of(c, chosen):
        shape = (parts_count, row_counts[c], size)
        return atom_sums(atoms, weights, sources[c], chosen, wide, owner_count, shape)

    parts = []
    if modes == 2:
        for c in range(len(row_counts)):
            if c > 0:
                sources[c], merged = lax.optimization_barrier((sources[c], merged))
                parts[-1][2] = lax.ppermute(merged, "energy", even_odd(2))
            relay, early = sums_of(c, (1, 2))
            if c > 0:
                relay, early, parts[-1][0] = lax.optimization_barrier((relay, early, parts[-1][0]))
            near, late = sums_of(c, (0, 3))
            relay = lax.ppermute(relay, "energy", inner(1))
            early = lax.ppermute(early, "energy", even_odd(-2))
            if c > 0:
                done = parts[-1][0].astype(f32) + parts[-1][2].astype(f32)
                relay, done = lax.optimization_barrier((relay, done))
                parts[-1][0], parts[-1][2] = done, jnp.zeros((), f32)
            late = (late + relay.astype(f32)).astype(bf16)
            near = lax.ppermute(near, "energy", inner(1))
            merged = late
            parts.append([early, near, None])
        parts[-1][2] = lax.ppermute(merged, "energy", even_odd(2))
        parts = [sum(x.astype(f32) for x in part).astype(bf16) for part in parts]
    else:
        for c in range(len(row_counts)):
            sums = sums_of(c, tuple(range(kinds)))
            up, down = sums[-2:]
            part = 0.0
            for d in range(1, modes):
                near = lax.ppermute(sums[2 * d - 2], "energy", inner(d))
                relay = lax.ppermute(sums[2 * d - 1], "energy", inner(d)).astype(f32)
                part = part + near.astype(f32)
                up = up + jnp.where(member < d, relay, 0.0)
                down = down + jnp.where(member < d, 0.0, relay)
            up = lax.ppermute(up.astype(bf16), "energy", outer(1))
            down = lax.ppermute(down.astype(bf16), "energy", outer(-1))
            parts.append((part + up.astype(f32) + down.astype(f32)).astype(bf16))
    return jnp.concatenate(parts, axis=3)


def solution(mesh):
    placed = (
        P("atom", "energy", None, None, None),
        P("atom", None, None, None, None),
        P(None, "atom", None),
        P("atom", None),
        P("atom"),
    )
    return jax.shard_map(
        body,
        mesh=mesh,
        in_specs=placed,
        out_specs=P("atom", "energy", None, None, None),
        check_vma=False,
    )
```

```python
import functools

import jax
import jax.numpy as jnp
from jax import lax
from jax.experimental import pallas as pl
from jax.experimental.pallas import tpu as pltpu
from jax.sharding import PartitionSpec as P

A_DEV = 8
SHARES = (4, 4)
VMEM_LIMIT = 52 * 2**20
PIECES = 3


def product_kernel(row_counts, capacity, split, atom_ref, green_ref, coupling_ref, *refs):
    outs, used_ref = refs[:-1], refs[-1]
    step = pl.program_id(0)
    group, components, _, size, _ = coupling_ref.shape
    my_owner = lax.axis_index("atom") if split else 0

    @pl.when(step == 0)
    def _():
        for owner in range(used_ref.shape[0]):
            used_ref[owner] = 0

    products = []
    for index in range(group):
        real_green = green_ref[index, 0, 0]
        imag_green = green_ref[index, 0, 1]
        right = jnp.concatenate(
            [
                jnp.concatenate([real_green, imag_green], axis=1),
                jnp.concatenate([-imag_green, real_green], axis=1),
            ],
            axis=0,
        )
        left = jnp.concatenate(
            [
                jnp.concatenate([coupling_ref[index, c, 0], coupling_ref[index, c, 1]], axis=1)
                for c in range(components)
            ],
            axis=0,
        )
        product = jnp.dot(left, right, preferred_element_type=jnp.float32).astype(jnp.bfloat16)
        products.append(
            jnp.concatenate([product[c * size : (c + 1) * size] for c in range(components)], axis=1)
        )
    for index in range(group):
        rows_of = []
        for c in range(components):
            real_last, imag_last = coupling_ref[index, c, 0].T, coupling_ref[index, c, 1].T
            rows_of.append(jnp.concatenate([real_last, imag_last], axis=1))
            rows_of.append(jnp.concatenate([-imag_last, real_last], axis=1))
        last = jnp.concatenate(rows_of, axis=0)
        total = lax.dot_general(
            products[index], last, (((1,), (0,)), ((), ())), preferred_element_type=jnp.float32
        ).astype(jnp.bfloat16)
        owner = lax.div(atom_ref[step * group + index], A_DEV)
        rank = used_ref[owner]
        used_ref[owner] = rank + 1
        near_place = (owner ^ my_owner) * capacity + rank
        first = 0
        for out, rows in zip(outs, row_counts):
            place = near_place if out is outs[0] else owner * capacity + rank
            out[place, 0] = total[first : first + rows, :size]
            out[place, 1] = total[first : first + rows, size:]
            first += rows


def bond_products(bond_atom, green, coupling, owner_count, capacity, row_counts, split):
    bond_count, _, parts, size, _ = green.shape
    components = coupling.shape[1]
    group = 8 if bond_count % 8 == 0 else 1
    return pl.pallas_call(
        functools.partial(product_kernel, row_counts, capacity, split),
        out_shape=[
            jax.ShapeDtypeStruct((owner_count * capacity, parts, rows, size), jnp.bfloat16)
            for rows in row_counts
        ],
        grid=(bond_count // group,),
        in_specs=[
            pl.BlockSpec(memory_space=pltpu.SMEM),
            pl.BlockSpec((group, 1, parts, size, size), lambda s: (s, 0, 0, 0, 0)),
            pl.BlockSpec((group, components, parts, size, size), lambda s: (s, 0, 0, 0, 0)),
        ],
        out_specs=[pl.BlockSpec(memory_space=pltpu.VMEM)] * len(row_counts),
        scratch_shapes=[pltpu.SMEM((owner_count,), jnp.int32)],
        compiler_params=pltpu.CompilerParams(vmem_limit_bytes=VMEM_LIMIT),
        cost_estimate=pl.CostEstimate(
            flops=16 * bond_count * components * size**3,
            bytes_accessed=2 * (green.size + coupling.size),
            transcendentals=0,
        ),
        name="bond_products",
    )(bond_atom, green, coupling)


def gather_kernel(kinds, owner_count, capacity, split, atom_ref, weight_ref, *refs):
    sources, outs, total = refs[: -len(kinds) - 1], refs[-len(kinds) - 1 : -1], refs[-1]
    rows = total.shape[2]
    slot_count = atom_ref.shape[0]
    total[...] = jnp.zeros_like(total)

    def add_owner(owner, source, first_slot):
        def add(slot, carry):
            entry = owner * capacity + slot
            atom = atom_ref[entry]
            start = pl.multiple_of((first_slot + slot) * rows, rows)
            values = source[pl.ds(start, rows), :].astype(jnp.float32)
            for index, kind in enumerate(kinds):
                total[index, atom] += weight_ref[kind * slot_count + entry] * values
            return carry

        @pl.when(atom_ref[owner * capacity] >= 0)
        def _():
            lax.fori_loop(0, capacity, add, 0, unroll=True)

    if len(sources) == owner_count:
        for owner, source in enumerate(sources):
            add_owner(owner, source, 0)
    else:

        me = lax.axis_index("atom") if split else 0

        def add_all(owner, carry):
            add_owner(owner, sources[0], (owner ^ me) * capacity)
            return carry

        lax.fori_loop(0, owner_count, add_all, 0)
    for index, out in enumerate(outs):
        out[...] = total[index].reshape(out.shape).astype(out.dtype)


def atom_sums(atoms, weights, sources, kinds, wide, owner_count, block_shape):
    capacity = atoms.shape[0] // owner_count
    parts, rows, size = block_shape
    return pl.pallas_call(
        functools.partial(gather_kernel, kinds, owner_count, capacity, owner_count == 4),
        out_shape=[
            jax.ShapeDtypeStruct(
                (A_DEV, 1, parts, rows, size), jnp.float32 if kind in wide else jnp.bfloat16
            )
            for kind in kinds
        ],
        grid_spec=pltpu.PrefetchScalarGridSpec(
            num_scalar_prefetch=2,
            grid=(1,),
            in_specs=[pl.BlockSpec(memory_space=pltpu.VMEM)] * len(sources),
            out_specs=[pl.BlockSpec(memory_space=pltpu.VMEM)] * len(kinds),
            scratch_shapes=[pltpu.VMEM((len(kinds), A_DEV, parts * rows, size), jnp.float32)],
        ),
        compiler_params=pltpu.CompilerParams(vmem_limit_bytes=32 * 2**20),
        cost_estimate=pl.CostEstimate(
            flops=2 * len(kinds) * len(sources) * sources[0].size,
            bytes_accessed=2 * len(sources) * sources[0].size,
            transcendentals=0,
        ),
        name="atom_sums",
    )(atoms, weights, *sources)


def body(green_blocks, coupling, phonon_weight, offsets, bond_atom):
    f32, bf16 = jnp.float32, jnp.bfloat16
    bond_count = green_blocks.shape[0]
    parts_count, size = green_blocks.shape[2], green_blocks.shape[-1]
    modes = offsets.shape[1]
    energy_size = lax.axis_size("energy")
    owner_count = lax.axis_size("atom")
    member = lax.axis_index("energy") % modes
    capacity = max(2, 2 * bond_count // owner_count)
    split = owner_count == 4
    slot_count = owner_count * capacity
    row_counts = [size * share // sum(SHARES) for share in SHARES]

    def inner(d):
        return [(e, e // modes * modes + (e + d) % modes) for e in range(energy_size)]

    def outer(d):
        return [(e, (e + d * modes) % energy_size) for e in range(energy_size)]

    def even_odd(step):
        return [(e, (e + (step if e % 2 == 0 else -step)) % energy_size) for e in range(energy_size)]

    products = bond_products(
        bond_atom, green_blocks, coupling, owner_count, capacity, row_counts, split
    )

    phonon_weight, offsets, bond_atom, products = lax.optimization_barrier(
        (phonon_weight, offsets, bond_atom, products)
    )
    if modes == 2:
        sign = jnp.where(member == 0, 1, -1)
        shifts = [sign, -sign, -2 * sign, 2 * sign]
        wide = (3,)
    else:
        shifts = []
        for d in range(1, modes):
            partner = (member + d) % modes
            shifts.append(partner - member)
            shifts.append(jnp.where(member > partner, modes, -modes) + partner - member)
        wide = (len(shifts), len(shifts) + 1)
        shifts += [jnp.int32(modes), jnp.int32(-modes)]
    kinds = len(shifts)
    owner_index = bond_atom // A_DEV
    bond_order = jnp.arange(bond_count, dtype=jnp.int32)
    same_owner = (owner_index[None, :] == owner_index[:, None]) & (
        bond_order[None, :] < bond_order[:, None]
    )
    rank = jnp.sum(same_owner.astype(jnp.int32), axis=1)
    route = owner_index ^ lax.axis_index("atom") if split else owner_index
    bond_weight = jnp.stack(
        [
            jnp.sum(
                jnp.where(
                    offsets == jnp.abs(shift),
                    jnp.where(shift > 0, phonon_weight[0], phonon_weight[1]),
                    0.0,
                ),
                axis=1,
            )
            for shift in shifts
        ],
        axis=1,
    )
    pieces, rest = [], bond_weight
    for piece in range(PIECES):
        pieces.append(lax.reduce_precision(rest, 8, 7))
        rest = rest - pieces[-1]
    facts = jnp.concatenate(pieces + [(bond_atom % A_DEV + 1).astype(f32)[:, None]], axis=1)
    slot_match = (route * capacity + rank)[None, :] == jnp.arange(slot_count)[:, None]
    facts = jnp.sum(jnp.where(slot_match[:, :, None], facts[None], 0.0), axis=1)
    facts = facts.astype(bf16).reshape(owner_count, capacity, -1)
    if split:
        facts = jnp.pad(
            facts, ((0, 0), (0, -capacity % 16), (0, size - facts.shape[2]))
        )
    else:
        facts = lax.all_to_all(facts, "atom", split_axis=0, concat_axis=0, tiled=True)

    def to_owners(blocks, facts):
        if not split or facts is None:
            blocks = blocks.reshape((owner_count, capacity) + blocks.shape[1:])
            blocks = lax.all_to_all(blocks, "atom", split_axis=0, concat_axis=0, tiled=True)
            return [blocks.reshape(-1, size)]
        blocks = blocks.reshape(owner_count, -1, size)
        if facts is not None:
            blocks = jnp.concatenate([blocks, facts], axis=1)
        return [blocks[0]] + [
            lax.ppermute(blocks[d], "atom", [(o, o ^ d) for o in range(owner_count)])
            for d in range(1, owner_count)
        ]

    sources = [
        to_owners(block, facts if c == 0 else None) for c, block in enumerate(products)
    ]
    if split:
        first = capacity * parts_count * row_counts[0]
        facts = jnp.concatenate([source[first : first + capacity] for source in sources[0]], axis=0)
    else:
        facts = facts.reshape(slot_count, -1)
    weights = sum(
        facts[:, piece * kinds : (piece + 1) * kinds].astype(f32) for piece in range(PIECES)
    )
    weights = weights.T.reshape(-1)
    atoms = facts[:, PIECES * kinds].astype(jnp.int32) - 1

    def sums_of(c, chosen):
        shape = (parts_count, row_counts[c], size)
        return atom_sums(atoms, weights, sources[c], chosen, wide, owner_count, shape)

    parts = []
    if modes == 2:
        for c in range(len(row_counts)):
            if c > 0:
                sources[c], merged = lax.optimization_barrier((sources[c], merged))
                parts[-1][2] = lax.ppermute(merged, "energy", even_odd(2))
            relay, early = sums_of(c, (1, 2))
            if c > 0:
                relay, early, parts[-1][0] = lax.optimization_barrier((relay, early, parts[-1][0]))
            near, late = sums_of(c, (0, 3))
            relay = lax.ppermute(relay, "energy", inner(1))
            early = lax.ppermute(early, "energy", even_odd(-2))
            if c > 0:
                done = parts[-1][0].astype(f32) + parts[-1][2].astype(f32)
                relay, done = lax.optimization_barrier((relay, done))
                parts[-1][0], parts[-1][2] = done, jnp.zeros((), f32)
            late = (late + relay.astype(f32)).astype(bf16)
            near = lax.ppermute(near, "energy", inner(1))
            merged = late
            parts.append([early, near, None])
        parts[-1][2] = lax.ppermute(merged, "energy", even_odd(2))
        parts = [sum(x.astype(f32) for x in part).astype(bf16) for part in parts]
    else:
        for c in range(len(row_counts)):
            sums = sums_of(c, tuple(range(kinds)))
            up, down = sums[-2:]
            part = 0.0
            for d in range(1, modes):
                near = lax.ppermute(sums[2 * d - 2], "energy", inner(d))
                relay = lax.ppermute(sums[2 * d - 1], "energy", inner(d)).astype(f32)
                part = part + near.astype(f32)
                up = up + jnp.where(member < d, relay, 0.0)
                down = down + jnp.where(member < d, 0.0, relay)
            up = lax.ppermute(up.astype(bf16), "energy", outer(1))
            down = lax.ppermute(down.astype(bf16), "energy", outer(-1))
            parts.append((part + up.astype(f32) + down.astype(f32)).astype(bf16))
    return jnp.concatenate(parts, axis=3)


def solution(mesh):
    placed = (
        P("atom", "energy", None, None, None),
        P("atom", None, None, None, None),
        P(None, "atom", None),
        P("atom", None),
        P("atom"),
    )
    return jax.shard_map(
        body,
        mesh=mesh,
        in_specs=placed,
        out_specs=P("atom", "energy", None, None, None),
        check_vma=False,
    )
```

```python
import functools

import jax
import jax.numpy as jnp
from jax import lax
from jax.experimental import pallas as pl
from jax.experimental.pallas import tpu as pltpu
from jax.sharding import PartitionSpec as P

A_DEV = 8
SHARES = (4, 4)
VMEM_LIMIT = 52 * 2**20
PIECES = 3


def product_kernel(row_counts, capacity, split, atom_ref, green_ref, coupling_ref, *refs):
    outs, used_ref = refs[:-1], refs[-1]
    step = pl.program_id(0)
    group, components, _, size, _ = coupling_ref.shape
    my_owner = lax.axis_index("atom") if split else 0

    @pl.when(step == 0)
    def _():
        for owner in range(used_ref.shape[0]):
            used_ref[owner] = 0

    products, lasts = [], []
    for index in range(group):
        real_green = green_ref[index, 0, 0]
        imag_green = green_ref[index, 0, 1]
        right = jnp.concatenate(
            [
                jnp.concatenate([real_green, imag_green], axis=1),
                jnp.concatenate([-imag_green, real_green], axis=1),
            ],
            axis=0,
        )
        left = jnp.concatenate(
            [
                jnp.concatenate([coupling_ref[index, c, 0], coupling_ref[index, c, 1]], axis=1)
                for c in range(components)
            ],
            axis=0,
        )
        product = jnp.dot(left, right, preferred_element_type=jnp.float32).astype(jnp.bfloat16)
        products.append(
            jnp.concatenate([product[c * size : (c + 1) * size] for c in range(components)], axis=1)
        )
        rows_of = []
        for c in range(components):
            real_last, imag_last = coupling_ref[index, c, 0].T, coupling_ref[index, c, 1].T
            rows_of.append(jnp.concatenate([real_last, imag_last], axis=1))
            rows_of.append(jnp.concatenate([-imag_last, real_last], axis=1))
        lasts.append(jnp.concatenate(rows_of, axis=0))
    for index in range(group):
        total = lax.dot_general(
            products[index], lasts[index], (((1,), (0,)), ((), ())), preferred_element_type=jnp.float32
        ).astype(jnp.bfloat16)
        owner = lax.div(atom_ref[step * group + index], A_DEV)
        rank = used_ref[owner]
        used_ref[owner] = rank + 1
        near_place = (owner ^ my_owner) * capacity + rank
        first = 0
        for out, rows in zip(outs, row_counts):
            place = near_place if out is outs[0] else owner * capacity + rank
            out[place, 0] = total[first : first + rows, :size]
            out[place, 1] = total[first : first + rows, size:]
            first += rows


def bond_products(bond_atom, green, coupling, owner_count, capacity, row_counts, split):
    bond_count, _, parts, size, _ = green.shape
    components = coupling.shape[1]
    group = 8 if bond_count % 8 == 0 else 1
    return pl.pallas_call(
        functools.partial(product_kernel, row_counts, capacity, split),
        out_shape=[
            jax.ShapeDtypeStruct((owner_count * capacity, parts, rows, size), jnp.bfloat16)
            for rows in row_counts
        ],
        grid=(bond_count // group,),
        in_specs=[
            pl.BlockSpec(memory_space=pltpu.SMEM),
            pl.BlockSpec((group, 1, parts, size, size), lambda s: (s, 0, 0, 0, 0)),
            pl.BlockSpec((group, components, parts, size, size), lambda s: (s, 0, 0, 0, 0)),
        ],
        out_specs=[pl.BlockSpec(memory_space=pltpu.VMEM)] * len(row_counts),
        scratch_shapes=[pltpu.SMEM((owner_count,), jnp.int32)],
        compiler_params=pltpu.CompilerParams(vmem_limit_bytes=VMEM_LIMIT),
        cost_estimate=pl.CostEstimate(
            flops=16 * bond_count * components * size**3,
            bytes_accessed=2 * (green.size + coupling.size),
            transcendentals=0,
        ),
        name="bond_products",
    )(bond_atom, green, coupling)


def gather_kernel(kinds, owner_count, capacity, split, atom_ref, weight_ref, *refs):
    sources, outs, total = refs[: -len(kinds) - 1], refs[-len(kinds) - 1 : -1], refs[-1]
    rows = total.shape[2]
    slot_count = atom_ref.shape[0]
    total[...] = jnp.zeros_like(total)

    def add_owner(owner, source, first_slot):
        def add(slot, carry):
            entry = owner * capacity + slot
            atom = atom_ref[entry]
            start = pl.multiple_of((first_slot + slot) * rows, rows)
            values = source[pl.ds(start, rows), :].astype(jnp.float32)
            for index, kind in enumerate(kinds):
                total[index, atom] += weight_ref[kind * slot_count + entry] * values
            return carry

        @pl.when(atom_ref[owner * capacity] >= 0)
        def _():
            lax.fori_loop(0, capacity, add, 0, unroll=True)

    if len(sources) == owner_count:
        for owner, source in enumerate(sources):
            add_owner(owner, source, 0)
    else:

        me = lax.axis_index("atom") if split else 0

        def add_all(owner, carry):
            add_owner(owner, sources[0], (owner ^ me) * capacity)
            return carry

        lax.fori_loop(0, owner_count, add_all, 0)
    for index, out in enumerate(outs):
        out[...] = total[index].reshape(out.shape).astype(out.dtype)


def atom_sums(atoms, weights, sources, kinds, wide, owner_count, block_shape):
    capacity = atoms.shape[0] // owner_count
    parts, rows, size = block_shape
    return pl.pallas_call(
        functools.partial(gather_kernel, kinds, owner_count, capacity, owner_count == 4),
        out_shape=[
            jax.ShapeDtypeStruct(
                (A_DEV, 1, parts, rows, size), jnp.float32 if kind in wide else jnp.bfloat16
            )
            for kind in kinds
        ],
        grid_spec=pltpu.PrefetchScalarGridSpec(
            num_scalar_prefetch=2,
            grid=(1,),
            in_specs=[pl.BlockSpec(memory_space=pltpu.VMEM)] * len(sources),
            out_specs=[pl.BlockSpec(memory_space=pltpu.VMEM)] * len(kinds),
            scratch_shapes=[pltpu.VMEM((len(kinds), A_DEV, parts * rows, size), jnp.float32)],
        ),
        compiler_params=pltpu.CompilerParams(vmem_limit_bytes=32 * 2**20),
        cost_estimate=pl.CostEstimate(
            flops=2 * len(kinds) * len(sources) * sources[0].size,
            bytes_accessed=2 * len(sources) * sources[0].size,
            transcendentals=0,
        ),
        name="atom_sums",
    )(atoms, weights, *sources)


def body(green_blocks, coupling, phonon_weight, offsets, bond_atom):
    f32, bf16 = jnp.float32, jnp.bfloat16
    bond_count = green_blocks.shape[0]
    parts_count, size = green_blocks.shape[2], green_blocks.shape[-1]
    modes = offsets.shape[1]
    energy_size = lax.axis_size("energy")
    owner_count = lax.axis_size("atom")
    member = lax.axis_index("energy") % modes
    capacity = max(2, 2 * bond_count // owner_count)
    split = owner_count == 4
    slot_count = owner_count * capacity
    row_counts = [size * share // sum(SHARES) for share in SHARES]

    def inner(d):
        return [(e, e // modes * modes + (e + d) % modes) for e in range(energy_size)]

    def outer(d):
        return [(e, (e + d * modes) % energy_size) for e in range(energy_size)]

    def even_odd(step):
        return [(e, (e + (step if e % 2 == 0 else -step)) % energy_size) for e in range(energy_size)]

    products = bond_products(
        bond_atom, green_blocks, coupling, owner_count, capacity, row_counts, split
    )

    phonon_weight, offsets, bond_atom, products = lax.optimization_barrier(
        (phonon_weight, offsets, bond_atom, products)
    )
    if modes == 2:
        sign = jnp.where(member == 0, 1, -1)
        shifts = [sign, -sign, -2 * sign, 2 * sign]
        wide = (3,)
    else:
        shifts = []
        for d in range(1, modes):
            partner = (member + d) % modes
            shifts.append(partner - member)
            shifts.append(jnp.where(member > partner, modes, -modes) + partner - member)
        wide = (len(shifts), len(shifts) + 1)
        shifts += [jnp.int32(modes), jnp.int32(-modes)]
    kinds = len(shifts)
    owner_index = bond_atom // A_DEV
    bond_order = jnp.arange(bond_count, dtype=jnp.int32)
    same_owner = (owner_index[None, :] == owner_index[:, None]) & (
        bond_order[None, :] < bond_order[:, None]
    )
    rank = jnp.sum(same_owner.astype(jnp.int32), axis=1)
    route = owner_index ^ lax.axis_index("atom") if split else owner_index
    bond_weight = jnp.stack(
        [
            jnp.sum(
                jnp.where(
                    offsets == jnp.abs(shift),
                    jnp.where(shift > 0, phonon_weight[0], phonon_weight[1]),
                    0.0,
                ),
                axis=1,
            )
            for shift in shifts
        ],
        axis=1,
    )
    pieces, rest = [], bond_weight
    for piece in range(PIECES):
        pieces.append(lax.reduce_precision(rest, 8, 7))
        rest = rest - pieces[-1]
    facts = jnp.concatenate(pieces + [(bond_atom % A_DEV + 1).astype(f32)[:, None]], axis=1)
    slot_match = (route * capacity + rank)[None, :] == jnp.arange(slot_count)[:, None]
    facts = jnp.sum(jnp.where(slot_match[:, :, None], facts[None], 0.0), axis=1)
    facts = facts.astype(bf16).reshape(owner_count, capacity, -1)
    if split:
        facts = jnp.pad(
            facts, ((0, 0), (0, -capacity % 16), (0, size - facts.shape[2]))
        )
    else:
        facts = lax.all_to_all(facts, "atom", split_axis=0, concat_axis=0, tiled=True)

    def to_owners(blocks, facts):
        if not split or facts is None:
            blocks = blocks.reshape((owner_count, capacity) + blocks.shape[1:])
            blocks = lax.all_to_all(blocks, "atom", split_axis=0, concat_axis=0, tiled=True)
            return [blocks.reshape(-1, size)]
        blocks = blocks.reshape(owner_count, -1, size)
        if facts is not None:
            blocks = jnp.concatenate([blocks, facts], axis=1)
        return [blocks[0]] + [
            lax.ppermute(blocks[d], "atom", [(o, o ^ d) for o in range(owner_count)])
            for d in range(1, owner_count)
        ]

    sources = [
        to_owners(block, facts if c == 0 else None) for c, block in enumerate(products)
    ]
    if split:
        first = capacity * parts_count * row_counts[0]
        facts = jnp.concatenate([source[first : first + capacity] for source in sources[0]], axis=0)
    else:
        facts = facts.reshape(slot_count, -1)
    weights = sum(
        facts[:, piece * kinds : (piece + 1) * kinds].astype(f32) for piece in range(PIECES)
    )
    weights = weights.T.reshape(-1)
    atoms = facts[:, PIECES * kinds].astype(jnp.int32) - 1

    def sums_of(c, chosen):
        shape = (parts_count, row_counts[c], size)
        return atom_sums(atoms, weights, sources[c], chosen, wide, owner_count, shape)

    parts = []
    if modes == 2:
        for c in range(len(row_counts)):
            if c > 0:
                sources[c], merged = lax.optimization_barrier((sources[c], merged))
                parts[-1][2] = lax.ppermute(merged, "energy", even_odd(2))
            relay, early = sums_of(c, (1, 2))
            if c > 0:
                early, parts[-1][0] = lax.optimization_barrier((early, parts[-1][0]))
            near, late = sums_of(c, (0, 3))
            relay = lax.ppermute(relay, "energy", inner(1))
            early = lax.ppermute(early, "energy", even_odd(-2))
            if c > 0:
                done = parts[-1][0].astype(f32) + parts[-1][2].astype(f32)
                relay, done = lax.optimization_barrier((relay, done))
                parts[-1][0], parts[-1][2] = done, jnp.zeros((), f32)
            late = (late + relay.astype(f32)).astype(bf16)
            near = lax.ppermute(near, "energy", inner(1))
            merged = late
            parts.append([early, near, None])
        parts[-1][2] = lax.ppermute(merged, "energy", even_odd(2))
        parts = [sum(x.astype(f32) for x in part).astype(bf16) for part in parts]
    else:
        for c in range(len(row_counts)):
            sums = sums_of(c, tuple(range(kinds)))
            up, down = sums[-2:]
            part = 0.0
            for d in range(1, modes):
                near = lax.ppermute(sums[2 * d - 2], "energy", inner(d))
                relay = lax.ppermute(sums[2 * d - 1], "energy", inner(d)).astype(f32)
                part = part + near.astype(f32)
                up = up + jnp.where(member < d, relay, 0.0)
                down = down + jnp.where(member < d, 0.0, relay)
            up = lax.ppermute(up.astype(bf16), "energy", outer(1))
            down = lax.ppermute(down.astype(bf16), "energy", outer(-1))
            parts.append((part + up.astype(f32) + down.astype(f32)).astype(bf16))
    return jnp.concatenate(parts, axis=3)


def solution(mesh):
    placed = (
        P("atom", "energy", None, None, None),
        P("atom", None, None, None, None),
        P(None, "atom", None),
        P("atom", None),
        P("atom"),
    )
    return jax.shard_map(
        body,
        mesh=mesh,
        in_specs=placed,
        out_specs=P("atom", "energy", None, None, None),
        check_vma=False,
    )
```

```python
import functools

import jax
import jax.numpy as jnp
from jax import lax
from jax.experimental import pallas as pl
from jax.experimental.pallas import tpu as pltpu
from jax.sharding import PartitionSpec as P

A_DEV = 8
SHARES = (4, 4)
VMEM_LIMIT = 52 * 2**20
PIECES = 3


def product_kernel(row_counts, capacity, split, atom_ref, green_ref, coupling_ref, *refs):
    outs, used_ref = refs[:-1], refs[-1]
    step = pl.program_id(0)
    group, components, _, size, _ = coupling_ref.shape
    my_owner = lax.axis_index("atom") if split else 0

    @pl.when(step == 0)
    def _():
        for owner in range(used_ref.shape[0]):
            used_ref[owner] = 0

    products, lasts = [], []
    for index in range(group):
        real_green = green_ref[index, 0, 0]
        imag_green = green_ref[index, 0, 1]
        right = jnp.concatenate(
            [
                jnp.concatenate([real_green, imag_green], axis=1),
                jnp.concatenate([-imag_green, real_green], axis=1),
            ],
            axis=0,
        )
        left = jnp.concatenate(
            [
                jnp.concatenate([coupling_ref[index, c, 0], coupling_ref[index, c, 1]], axis=1)
                for c in range(components)
            ],
            axis=0,
        )
        product = jnp.dot(left, right, preferred_element_type=jnp.float32).astype(jnp.bfloat16)
        products.append(
            jnp.concatenate([product[c * size : (c + 1) * size] for c in range(components)], axis=1)
        )
        rows_of = []
        for c in range(components):
            real_last, imag_last = coupling_ref[index, c, 0].T, coupling_ref[index, c, 1].T
            rows_of.append(jnp.concatenate([real_last, imag_last], axis=1))
            rows_of.append(jnp.concatenate([-imag_last, real_last], axis=1))
        lasts.append(jnp.concatenate(rows_of, axis=0))
    for index in range(group):
        total = lax.dot_general(
            products[index], lasts[index], (((1,), (0,)), ((), ())), preferred_element_type=jnp.float32
        ).astype(jnp.bfloat16)
        owner = lax.div(atom_ref[step * group + index], A_DEV)
        rank = used_ref[owner]
        used_ref[owner] = rank + 1
        near_place = (owner ^ my_owner) * capacity + rank
        first = 0
        for out, rows in zip(outs, row_counts):
            place = near_place if out is outs[0] else owner * capacity + rank
            out[place, 0] = total[first : first + rows, :size]
            out[place, 1] = total[first : first + rows, size:]
            first += rows


def bond_products(bond_atom, green, coupling, owner_count, capacity, row_counts, split):
    bond_count, _, parts, size, _ = green.shape
    components = coupling.shape[1]
    group = 8 if bond_count % 8 == 0 else 1
    return pl.pallas_call(
        functools.partial(product_kernel, row_counts, capacity, split),
        out_shape=[
            jax.ShapeDtypeStruct((owner_count * capacity, parts, rows, size), jnp.bfloat16)
            for rows in row_counts
        ],
        grid=(bond_count // group,),
        in_specs=[
            pl.BlockSpec(memory_space=pltpu.SMEM),
            pl.BlockSpec((group, 1, parts, size, size), lambda s: (s, 0, 0, 0, 0)),
            pl.BlockSpec((group, components, parts, size, size), lambda s: (s, 0, 0, 0, 0)),
        ],
        out_specs=[pl.BlockSpec(memory_space=pltpu.VMEM)] * len(row_counts),
        scratch_shapes=[pltpu.SMEM((owner_count,), jnp.int32)],
        compiler_params=pltpu.CompilerParams(vmem_limit_bytes=VMEM_LIMIT),
        cost_estimate=pl.CostEstimate(
            flops=16 * bond_count * components * size**3,
            bytes_accessed=2 * (green.size + coupling.size),
            transcendentals=0,
        ),
        name="bond_products",
    )(bond_atom, green, coupling)


def gather_kernel(kinds, owner_count, capacity, split, atom_ref, weight_ref, *refs):
    sources, outs, total = refs[: -len(kinds) - 1], refs[-len(kinds) - 1 : -1], refs[-1]
    rows = total.shape[2]
    slot_count = atom_ref.shape[0]
    total[...] = jnp.zeros_like(total)

    def add_owner(owner, source, first_slot):
        def add(slot, carry):
            entry = owner * capacity + slot
            atom = atom_ref[entry]
            start = pl.multiple_of((first_slot + slot) * rows, rows)
            values = source[pl.ds(start, rows), :].astype(jnp.float32)
            for index, kind in enumerate(kinds):
                total[index, atom] += weight_ref[kind * slot_count + entry] * values
            return carry

        @pl.when(atom_ref[owner * capacity] >= 0)
        def _():
            lax.fori_loop(0, capacity, add, 0, unroll=True)

    if len(sources) == owner_count:
        for owner, source in enumerate(sources):
            add_owner(owner, source, 0)
    else:

        me = lax.axis_index("atom") if split else 0

        def add_all(owner, carry):
            add_owner(owner, sources[0], (owner ^ me) * capacity)
            return carry

        lax.fori_loop(0, owner_count, add_all, 0)
    for index, out in enumerate(outs):
        out[...] = total[index].reshape(out.shape).astype(out.dtype)


def atom_sums(atoms, weights, sources, kinds, wide, owner_count, block_shape):
    capacity = atoms.shape[0] // owner_count
    parts, rows, size = block_shape
    return pl.pallas_call(
        functools.partial(gather_kernel, kinds, owner_count, capacity, owner_count == 4),
        out_shape=[
            jax.ShapeDtypeStruct(
                (A_DEV, 1, parts, rows, size), jnp.float32 if kind in wide else jnp.bfloat16
            )
            for kind in kinds
        ],
        grid_spec=pltpu.PrefetchScalarGridSpec(
            num_scalar_prefetch=2,
            grid=(1,),
            in_specs=[pl.BlockSpec(memory_space=pltpu.VMEM)] * len(sources),
            out_specs=[pl.BlockSpec(memory_space=pltpu.VMEM)] * len(kinds),
            scratch_shapes=[pltpu.VMEM((len(kinds), A_DEV, parts * rows, size), jnp.float32)],
        ),
        compiler_params=pltpu.CompilerParams(vmem_limit_bytes=32 * 2**20),
        cost_estimate=pl.CostEstimate(
            flops=2 * len(kinds) * len(sources) * sources[0].size,
            bytes_accessed=2 * len(sources) * sources[0].size,
            transcendentals=0,
        ),
        name="atom_sums",
    )(atoms, weights, *sources)


def body(green_blocks, coupling, phonon_weight, offsets, bond_atom):
    f32, bf16 = jnp.float32, jnp.bfloat16
    bond_count = green_blocks.shape[0]
    parts_count, size = green_blocks.shape[2], green_blocks.shape[-1]
    modes = offsets.shape[1]
    energy_size = lax.axis_size("energy")
    owner_count = lax.axis_size("atom")
    member = lax.axis_index("energy") % modes
    capacity = max(2, 2 * bond_count // owner_count)
    split = owner_count == 4
    slot_count = owner_count * capacity
    row_counts = [size * share // sum(SHARES) for share in SHARES]

    def inner(d):
        return [(e, e // modes * modes + (e + d) % modes) for e in range(energy_size)]

    def outer(d):
        return [(e, (e + d * modes) % energy_size) for e in range(energy_size)]

    def even_odd(step):
        return [(e, (e + (step if e % 2 == 0 else -step)) % energy_size) for e in range(energy_size)]

    products = bond_products(
        bond_atom, green_blocks, coupling, owner_count, capacity, row_counts, split
    )

    phonon_weight, offsets, bond_atom, products = lax.optimization_barrier(
        (phonon_weight, offsets, bond_atom, products)
    )
    if modes == 2:
        sign = jnp.where(member == 0, 1, -1)
        shifts = [sign, -sign, -2 * sign, 2 * sign]
        wide = (3,)
    else:
        shifts = []
        for d in range(1, modes):
            partner = (member + d) % modes
            shifts.append(partner - member)
            shifts.append(jnp.where(member > partner, modes, -modes) + partner - member)
        wide = (len(shifts), len(shifts) + 1)
        shifts += [jnp.int32(modes), jnp.int32(-modes)]
    kinds = len(shifts)
    owner_index = bond_atom // A_DEV
    bond_order = jnp.arange(bond_count, dtype=jnp.int32)
    same_owner = (owner_index[None, :] == owner_index[:, None]) & (
        bond_order[None, :] < bond_order[:, None]
    )
    rank = jnp.sum(same_owner.astype(jnp.int32), axis=1)
    route = owner_index ^ lax.axis_index("atom") if split else owner_index
    bond_weight = jnp.stack(
        [
            jnp.sum(
                jnp.where(
                    offsets == jnp.abs(shift),
                    jnp.where(shift > 0, phonon_weight[0], phonon_weight[1]),
                    0.0,
                ),
                axis=1,
            )
            for shift in shifts
        ],
        axis=1,
    )
    pieces, rest = [], bond_weight
    for piece in range(PIECES):
        pieces.append(lax.reduce_precision(rest, 8, 7))
        rest = rest - pieces[-1]
    facts = jnp.concatenate(pieces + [(bond_atom % A_DEV + 1).astype(f32)[:, None]], axis=1)
    slot_match = (route * capacity + rank)[None, :] == jnp.arange(slot_count)[:, None]
    facts = jnp.sum(jnp.where(slot_match[:, :, None], facts[None], 0.0), axis=1)
    facts = facts.astype(bf16).reshape(owner_count, capacity, -1)
    if split:
        facts = jnp.pad(
            facts, ((0, 0), (0, -capacity % 16), (0, size - facts.shape[2]))
        )
    else:
        facts = lax.all_to_all(facts, "atom", split_axis=0, concat_axis=0, tiled=True)

    def to_owners(blocks, facts):
        if not split or facts is None:
            blocks = blocks.reshape((owner_count, capacity) + blocks.shape[1:])
            blocks = lax.all_to_all(blocks, "atom", split_axis=0, concat_axis=0, tiled=True)
            return [blocks.reshape(-1, size)]
        blocks = blocks.reshape(owner_count, -1, size)
        if facts is not None:
            blocks = jnp.concatenate([blocks, facts], axis=1)
        return [blocks[0]] + [
            lax.ppermute(blocks[d], "atom", [(o, o ^ d) for o in range(owner_count)])
            for d in range(1, owner_count)
        ]

    sources = [
        to_owners(block, facts if c == 0 else None) for c, block in enumerate(products)
    ]
    if split:
        first = capacity * parts_count * row_counts[0]
        facts = jnp.concatenate([source[first : first + capacity] for source in sources[0]], axis=0)
    else:
        facts = facts.reshape(slot_count, -1)
    weights = sum(
        facts[:, piece * kinds : (piece + 1) * kinds].astype(f32) for piece in range(PIECES)
    )
    weights = weights.T.reshape(-1)
    atoms = facts[:, PIECES * kinds].astype(jnp.int32) - 1

    def sums_of(c, chosen):
        shape = (parts_count, row_counts[c], size)
        return atom_sums(atoms, weights, sources[c], chosen, wide, owner_count, shape)

    parts = []
    if modes == 2:
        for c in range(len(row_counts)):
            if c > 0:
                sources[c], merged = lax.optimization_barrier((sources[c], merged))
                parts[-1][2] = lax.ppermute(merged, "energy", even_odd(2))
            relay, early = sums_of(c, (1, 2))
            if c > 0:
                relay, early, parts[-1][0] = lax.optimization_barrier((relay, early, parts[-1][0]))
            near, late = sums_of(c, (0, 3))
            relay = lax.ppermute(relay, "energy", inner(1))
            early = lax.ppermute(early, "energy", even_odd(-2))
            if c > 0:
                done = parts[-1][0].astype(f32) + parts[-1][2].astype(f32)
                relay, done = lax.optimization_barrier((relay, done))
                parts[-1][0], parts[-1][2] = done, jnp.zeros((), f32)
            late = (late + relay.astype(f32)).astype(bf16)
            near = lax.ppermute(near, "energy", inner(1))
            merged = late
            parts.append([early, near, None])
        parts[-1][2] = lax.ppermute(merged, "energy", even_odd(2))
        parts = [sum(x.astype(f32) for x in part).astype(bf16) for part in parts]
    else:
        for c in range(len(row_counts)):
            sums = sums_of(c, tuple(range(kinds)))
            up, down = sums[-2:]
            part = 0.0
            for d in range(1, modes):
                near = lax.ppermute(sums[2 * d - 2], "energy", inner(d))
                relay = lax.ppermute(sums[2 * d - 1], "energy", inner(d)).astype(f32)
                part = part + near.astype(f32)
                up = up + jnp.where(member < d, relay, 0.0)
                down = down + jnp.where(member < d, 0.0, relay)
            up = lax.ppermute(up.astype(bf16), "energy", outer(1))
            down = lax.ppermute(down.astype(bf16), "energy", outer(-1))
            parts.append((part + up.astype(f32) + down.astype(f32)).astype(bf16))
    return jnp.concatenate(parts, axis=3)


def solution(mesh):
    placed = (
        P("atom", "energy", None, None, None),
        P("atom", None, None, None, None),
        P(None, "atom", None),
        P("atom", None),
        P("atom"),
    )
    return jax.shard_map(
        body,
        mesh=mesh,
        in_specs=placed,
        out_specs=P("atom", "energy", None, None, None),
        check_vma=False,
    )
```
